32 devices in a mesh: grp: 2 (over y), role: 2 (over core), ctx: 8 (over z, x).
Axes of the slice: x: 2, y: 2, z: 4, core: 2. Of those that a mesh axis runs over, the one named last changes fastest.
Arguments:
- teacher_streams: bfloat16 [3, 8192, 4096], P(None, ('grp', 'ctx'), 'role'), parts along dimension 1, may hold values from -6 to 6
- conv_filter: bfloat16 [4096, 128], P('role'), may hold values from -0.5 to 0.5
- map_weight: bfloat16 [4096, 2048], P(('role', 'ctx')), may hold values from -0.125 to 0.125
- bases: int32 [8192], P(('grp', 'ctx')), parts along dimension 0, may hold values from 0 to 3
- base_weights: float32 [4], replicated, may hold values from 0.25 to 2
- student_qkv: bfloat16 [3, 8192, 2048], P(None, ('grp', 'ctx'), 'role'), parts along dimension 1, may hold values from -6 to 6
Outputs:
- student_grads: bfloat16 [3, 8192, 2048], P(None, ('grp', 'ctx'), 'role'), parts along dimension 1
The draws below stay inside these ranges and needn't reach their ends.
There are 2 independent parts, one for each index of `grp`. The reference program is written for one: setup_inputs(seed, part) draws one part's arguments, and reference() takes and returns one part's arrays. A program takes and returns all parts, laid end to end along the dimension named above; an argument that names none is the same for every part. Nothing has to cross between parts.
All inputs are finite; a program needn't handle non-finite values.
Results may differ from the reference program's by a relative error of at most 0.0055.
Values may be sent and summed in bfloat16 or wider, within the bound.
A program may use at most 192 MiB of HBM per device.

```python
import math
import jax
import jax.numpy as jnp
from jax import lax

DT = 4096
TAPS = 128
DS = 2048
HEADS = 16
DH = 128
BLK = 512
SEQ = 4096


def set_ends(values, stream_key, smallest, largest):
    longest = values.shape.index(max(values.shape))
    spots = []
    for shift in (0, 1):
        where = [jax.random.randint(jax.random.fold_in(stream_key, axis), (), 0, length) for axis, length in enumerate(values.shape)]
        where[longest] = (where[longest] + shift) % values.shape[longest]
        spots.append(tuple(where))
    return values.at[spots[0]].set(smallest).at[spots[1]].set(largest)


def raised(result, stream_key, source, target, shards_of, factor):
    def block_of(position):
        return (jnp.arange(result.shape[position]) // (result.shape[position] // shards_of)).reshape((-1,) + (1,) * (result.ndim - 1 - position))

    first = jax.random.permutation(stream_key, shards_of)[block_of(target)]
    other_side = (block_of(target) + shards_of // 2) % shards_of
    return jnp.where((block_of(source) == first) | (block_of(source) == other_side), factor * result, result)


def block_levels(own_key, extent, pieces, low, largest):
    gain, own = 1.0, jax.random.fold_in(own_key, 6)
    for axis_at, blocks in pieces:
        heights = jnp.exp(jax.random.uniform(jax.random.fold_in(own, axis_at), (blocks,), jnp.float32, low / len(pieces), largest / len(pieces)))
        gain = gain * jnp.repeat(heights, extent[axis_at] // blocks).reshape([-1 if axis == axis_at else 1 for axis in range(len(extent))])
    return gain


def noise(stream_key, shape, spread, reach, shards=(), held_as=jnp.bfloat16):
    result = jax.random.normal(stream_key, shape, jnp.float32) * spread
    if len(shards) > 0:
        result = block_levels(stream_key, shape, shards, -0.22, 0.18) * result
    return jnp.clip(result, min=-reach, max=reach).astype(held_as)


def noise_with(rng, extent, deviation, bound, cuts, heavy, kind=jnp.bfloat16):
    drawn = deviation * jax.random.normal(rng, extent, jnp.float32)
    if cuts:
        drawn = drawn * block_levels(rng, extent, cuts, -0.22, 0.18)
    return jnp.clip(raised(drawn, jax.random.fold_in(rng, 3), *heavy), -bound, bound).astype(kind)


def setup_inputs(seed: int = 0, part: int = 0) -> dict:
    streams_of = jax.random.split(jax.random.key(seed), 7)
    own_keys = jax.random.split(jax.random.fold_in(streams_of[6], part), 7)
    teacher_streams = noise(own_keys[0], (3, SEQ, DT), 1.0, 6.0, ((1, 8), (2, 2)))
    conv_filter = noise(streams_of[1], (DT, TAPS), TAPS ** -0.5, 0.5, ((0, 2),))
    map_weight = noise_with(streams_of[2], (DT, DS), DT ** -0.5, 0.125, ((0, 16),), (0, 1, 16, 2.0))
    bases = set_ends(jax.random.randint(own_keys[3], (SEQ,), 0, 4), jax.random.fold_in(own_keys[3], 1), 0, 3).astype(jnp.int32)
    base_weights = jnp.clip(jnp.exp(jax.random.uniform(streams_of[4], (4,), jnp.float32, math.log(0.25), math.log(2.0))), 0.25, 2.0)
    student_qkv = noise(own_keys[5], (3, SEQ, DS), 1.0, 6.0, ((1, 8), (2, 2)))
    return {"teacher_streams": teacher_streams, "conv_filter": conv_filter, "map_weight": map_weight, "bases": bases, "base_weights": base_weights, "student_qkv": student_qkv}


def round_keep(values):
    return lax.optimization_barrier(values.astype(jnp.bfloat16)).astype(jnp.float32)


def reference(teacher_streams, conv_filter, map_weight, bases, base_weights, student_qkv):
    nblocks = SEQ // BLK
    filters_f = conv_filter.astype(jnp.float32)

    def teacher_block(rim, index):
        start = (index * BLK).astype(jnp.int32)
        gate_blk = lax.dynamic_slice_in_dim(teacher_streams[0], start, BLK, 0).astype(jnp.float32)
        key_blk = lax.dynamic_slice_in_dim(teacher_streams[1], start, BLK, 0).astype(jnp.float32)
        val_blk = lax.dynamic_slice_in_dim(teacher_streams[2], start, BLK, 0).astype(jnp.float32)
        mixed_blk = (key_blk * val_blk).astype(jnp.bfloat16)
        extended = jnp.concatenate([rim, mixed_blk], 0).astype(jnp.float32)

        def add_tap(tap, total):
            first = (TAPS - 1 - tap).astype(jnp.int32)
            window = lax.dynamic_slice_in_dim(extended, first, BLK, 0)
            column = lax.dynamic_slice_in_dim(filters_f, tap.astype(jnp.int32), 1, 1)[:, 0]
            return total + window * column[None, :]

        conv_out = lax.fori_loop(0, TAPS, add_tap, jnp.zeros((BLK, DT), jnp.float32))
        teacher_out = (gate_blk * conv_out).astype(jnp.bfloat16)
        target_blk = jnp.dot(teacher_out, map_weight, preferred_element_type=jnp.float32)
        return mixed_blk[BLK - (TAPS - 1):], target_blk

    rim_zero = jnp.zeros((TAPS - 1, DT), jnp.bfloat16)
    _, targets = lax.scan(teacher_block, rim_zero, jnp.arange(nblocks, dtype=jnp.int32))

    att_scale = float(DH * SEQ) ** -0.5
    queries = student_qkv[0].reshape(nblocks, BLK, HEADS, DH)
    keys_all = student_qkv[1].reshape(nblocks, BLK, HEADS, DH)
    values_all = student_qkv[2].reshape(nblocks, BLK, HEADS, DH)
    tok_weight = base_weights[bases].reshape(nblocks, BLK)
    causal = jnp.arange(BLK)[:, None] >= jnp.arange(BLK)[None, :]

    def forward(carried, block):
        q_blk, k_blk, v_blk = [x.astype(jnp.float32) for x in block[:3]]
        target_blk = block[3]
        weight_blk = block[4]
        prefix_bf = carried.astype(jnp.bfloat16)
        scores = jnp.einsum('thd,shd->hts', q_blk, k_blk)
        scores_bf = jnp.where(causal[None], scores, 0.0).astype(jnp.bfloat16)
        block_out = att_scale * (jnp.einsum('thd,hde->the', q_blk, prefix_bf.astype(jnp.float32)) + jnp.einsum('hts,she->the', scores_bf.astype(jnp.float32), v_blk))
        resid_blk = (weight_blk[:, None] * (block_out.reshape(BLK, DS) - target_blk)).astype(jnp.bfloat16)
        carried = carried + jnp.einsum('shd,she->hde', k_blk, v_blk)
        return carried, (resid_blk.reshape(BLK, HEADS, DH), prefix_bf)

    zero_state = jnp.zeros((HEADS, DH, DH), jnp.float32)
    _, (resid_bf, prefixes) = lax.scan(forward, zero_state, (queries, keys_all, values_all, targets, tok_weight))

    def backward(later_sum, block):
        q_blk, k_blk, v_blk, r_blk = [x.astype(jnp.float32) for x in block[:4]]
        prefix_f = block[4].astype(jnp.float32)
        later_f = round_keep(later_sum)
        scores = jnp.einsum('thd,shd->hts', q_blk, k_blk)
        scores_f = round_keep(jnp.where(causal[None], scores, 0.0))
        grad_scores = round_keep(jnp.where(causal[None], jnp.einsum('the,she->hts', r_blk, v_blk), 0.0))
        grad_query = att_scale * (jnp.einsum('the,hde->thd', r_blk, prefix_f) + jnp.einsum('hts,shd->thd', grad_scores, k_blk))
        grad_key = att_scale * (jnp.einsum('she,hde->shd', v_blk, later_f) + jnp.einsum('hts,thd->shd', grad_scores, q_blk))
        grad_value = att_scale * (jnp.einsum('shd,hde->she', k_blk, later_f) + jnp.einsum('hts,the->she', scores_f, r_blk))
        later_sum = later_sum + jnp.einsum('thd,the->hde', q_blk, r_blk)
        stacked = jnp.stack([grad_query.reshape(BLK, DS), grad_key.reshape(BLK, DS), grad_value.reshape(BLK, DS)], 0).astype(jnp.bfloat16)
        return later_sum, stacked

    _, grads = lax.scan(backward, zero_state, (queries, keys_all, values_all, resid_bf, prefixes), reverse=True)
    return jnp.moveaxis(grads, 1, 0).reshape(3, SEQ, DS)
```

```python
import functools

import jax
import jax.numpy as jnp
import ml_dtypes
import numpy as np
from jax import lax
from jax.experimental import pallas as pl
from jax.experimental.pallas import tpu as pltpu
from jax.sharding import PartitionSpec as P

DH = 128
LANE = 128
BF = jnp.bfloat16
F32 = jnp.float32
MESH = pl.DeviceIdType.MESH


def transform(taps):
    freq = np.arange(taps)[:, None]
    time = np.arange(2 * taps)[None, :]
    angle = np.pi * ((2 * freq + 1) * time % (4 * taps)) / (2 * taps)
    full = np.concatenate([np.cos(angle), -np.sin(angle)], 0)
    back = full[:, taps:].T / taps
    pieces = []
    for matrix in (full, back):
        high = matrix.astype(ml_dtypes.bfloat16)
        low = (matrix - high.astype(np.float64)).astype(ml_dtypes.bfloat16)
        pieces += [high, low]
    return pieces


def dot(a, b, dims=((1,), (0,))):
    return lax.dot_general(a, b, (dims, ((), ())), preferred_element_type=F32)


NT = ((1,), (1,))
TN = ((0,), (0,))


def kernel(
    n, nx, scale,
    streams, filt, wmap, tokw, qkv, fhi, flo, ghi, glo,
    grads,
    wcw, wccw, wy, xbuf, tbuf, tcw, tccw, ty, out, resid, own, exc, prefix, hsend, hrecv, bsend, brecv,
    in_loc, in_send, in_recv, cw_send, cw_recv, cc_send, cc_recv, y_send, y_recv,
    halo_send, halo_recv, t_send, t_recv, h_ssem, h_rsem, b_ssem, b_rsem,
):
    toks, chans = streams.shape[1], streams.shape[2]
    width = qkv.shape[2]
    heads = width // DH
    rows = wmap.shape[0]
    taps = filt.shape[1]
    rounds = hsend.shape[0]
    quarter = width // 4
    cwn = tcw.shape[1]
    common = width // 2
    g, r, me = lax.axis_index("grp"), lax.axis_index("role"), lax.axis_index("ctx")
    nz = n // nx

    def ctx_of(pos):
        pos = lax.rem(pos + n, n)
        x, t = lax.div(pos, nz), lax.rem(pos, nz)
        z = t + lax.rem(x, 2) * (nz - 1 - 2 * t)
        return z * nx + x

    z0, x0 = lax.div(me, nx), lax.rem(me, nx)
    pos = x0 * nz + z0 + lax.rem(x0, 2) * (nz - 1 - 2 * z0)
    nxt, prv = ctx_of(pos + 1), ctx_of(pos - 1)

    bar = pltpu.get_barrier_semaphore()
    for peer in ({"ctx": nxt}, {"ctx": prv}, {"grp": 1 - g}, {"role": 1 - r}):
        pl.semaphore_signal(bar, inc=1, device_id=peer, device_id_type=MESH)
    for k in range(rounds):
        d = 1 << k

        @pl.when(me + d < n)
        def _():
            pl.semaphore_signal(bar, inc=1, device_id={"ctx": me + d}, device_id_type=MESH)

        @pl.when(me >= d)
        def _():
            pl.semaphore_signal(bar, inc=1, device_id={"ctx": me - d}, device_id_type=MESH)

    peers = 4
    for k in range(rounds):
        d = 1 << k
        peers = peers + jnp.where(me + d < n, 1, 0) + jnp.where(me >= d, 1, 0)
    pl.semaphore_wait(bar, peers)

    def span(ctx):
        return pl.ds(pl.multiple_of(ctx * rows, 16), rows)

    def remote(src, dst, ssem, rsem, peer):
        return pltpu.make_async_remote_copy(
            src_ref=src, dst_ref=dst, send_sem=ssem, recv_sem=rsem, device_id=peer, device_id_type=MESH
        )

    def shares(role):
        base = role * width
        mine = base + g * quarter
        other = base + (1 - g) * quarter
        cols = lambda at, size: pl.ds(pl.multiple_of(at, LANE), size)
        return [
            (wmap.at[:, cols(base + common, cwn)], wcw.at[r, span(me), :]),
            (wmap.at[:, cols(base + common + cwn, LANE)], wccw.at[r, span(me), pl.ds(0, LANE)]),
            (wmap.at[:, cols(mine, quarter)], wccw.at[r, span(me), pl.ds(LANE, quarter)]),
            (wmap.at[:, cols(other, quarter)], wy.at[r, span(me), :]),
        ]

    first = [
        remote(src, dst, in_send.at[i], in_recv.at[i], {"role": 1 - r})
        for i, (src, dst) in enumerate(shares(1 - r))
    ]
    for copy in first:
        copy.start()
    local = [
        pltpu.make_async_copy(src, dst, in_loc.at[i]) for i, (src, dst) in enumerate(shares(r))
    ]
    for copy in local:
        copy.start()

    def cw_copy(s):
        at = span(ctx_of(pos - s))
        return remote(wcw.at[:, at, :], wcw.at[:, at, :], cw_send.at[s], cw_recv.at[s], {"ctx": nxt})

    def cw_in(s):
        at = span(ctx_of(pos - s))
        return remote(wcw.at[:, at, :], wcw.at[:, at, :], cw_send.at[s - 1], cw_recv.at[s - 1], {"ctx": nxt})

    def cc_copy(s):
        at = span(ctx_of(pos + s))
        return remote(wccw.at[:, at, :], wccw.at[:, at, :], cc_send.at[s], cc_recv.at[s], {"ctx": prv})

    def cc_in(s):
        at = span(ctx_of(pos + s))
        return remote(wccw.at[:, at, :], wccw.at[:, at, :], cc_send.at[s - 1], cc_recv.at[s - 1], {"ctx": prv})

    def y_copy(s):
        at = span(ctx_of(pos + s))
        return remote(
            wccw.at[:, at, pl.ds(LANE, quarter)], wy.at[:, at, :], y_send.at[s], y_recv.at[s], {"grp": 1 - g}
        )

    def ring_in(s):
        cw_in(s).wait_recv()
        cc_in(s).wait_recv()

        def onward():
            cw_copy(s).start()
            cc_copy(s).start()

        if isinstance(s, int):
            if s < n - 1:
                onward()
        else:
            pl.when(s < n - 1)(onward)
        y_copy(s).start()

    def mix():
        @pl.loop(0, toks // 128)
        def _(b):
            at = pl.ds(pl.multiple_of(b * 128, 128), 128)
            xbuf[pl.ds(pl.multiple_of(b * 128 + taps, 128), 128), :] = (
                streams[1, at, :].astype(F32) * streams[2, at, :].astype(F32)
            ).astype(BF)

    halo = remote(
        xbuf.at[pl.ds(toks, taps), :], xbuf.at[pl.ds(0, taps), :], halo_send, halo_recv, {"ctx": me + 1}
    )

    def head(h):
        return pl.ds(pl.multiple_of(h * DH, DH), DH)

    def scan_send(k, up, send, recv, ssem, rsem):
        d = 1 << k
        send[k] = (own[...] + exc[...]).astype(BF)

        @pl.when((me + d < n) if up else (me >= d))
        def _():
            scan_copy(k, up, send, recv, ssem, rsem).start()

    def scan_copy(k, up, send, recv, ssem, rsem):
        d = 1 << k
        return remote(send.at[k], recv.at[k], ssem.at[k], rsem.at[k], {"ctx": me + d if up else me - d})

    def scan_recv(k, up, send, recv, ssem, rsem):
        d = 1 << k

        @pl.when((me >= d) if up else (me + d < n))
        def _():
            scan_copy(k, up, send, recv, ssem, rsem).wait_recv()
            exc[...] += recv[k].astype(F32)

    def scan_done(k, up, send, recv, ssem, rsem):
        d = 1 << k

        @pl.when((me + d < n) if up else (me >= d))
        def _():
            scan_copy(k, up, send, recv, ssem, rsem).wait_send()

    fwd = (True, hsend, hrecv, h_ssem, h_rsem)
    bwd = (False, bsend, brecv, b_ssem, b_rsem)

    def own_state():
        exc[...] = jnp.zeros_like(exc)

        @pl.loop(0, heads)
        def _(h):
            own[h] = dot(qkv[1, :, head(h)], qkv[2, :, head(h)], TN)

    tile = 256

    def conv(blocks):
        @pl.loop(0, chans // tile)
        def _(c):
            cols = pl.ds(pl.multiple_of(c * tile, tile), tile)
            taps_c = filt[cols, :]
            hh = dot(fhi[:, :taps], taps_c, NT) + dot(flo[:, :taps], taps_c, NT)
            hr, hi = hh[:taps], hh[taps:]
            for b in blocks:
                x = xbuf[b * taps : (b + 2) * taps, cols]
                xx = dot(fhi[...], x) + dot(flo[...], x)
                xr, xi = xx[:taps], xx[taps:]
                y = jnp.concatenate([xr * hr - xi * hi, xr * hi + xi * hr], 0)
                yh = y.astype(BF)
                yl = (y - yh.astype(F32)).astype(BF)
                res = dot(ghi[...], yh) + dot(ghi[...], yl) + dot(glo[...], yh)
                at = pl.ds(b * taps, taps)
                tbuf[r, at, cols] = (streams[0, at, cols].astype(F32) * res).astype(BF)

    tcopy = remote(tbuf.at[r], tbuf.at[r], t_send, t_recv, {"role": 1 - r})

    def tri():
        return lax.broadcasted_iota(jnp.int32, (toks, toks), 0) >= lax.broadcasted_iota(
            jnp.int32, (toks, toks), 1
        )

    def forward():
        prefix[...] = exc[...].astype(BF)

        @pl.loop(0, heads)
        def _(h):
            q, k, v = qkv[0, :, head(h)], qkv[1, :, head(h)], qkv[2, :, head(h)]
            sc = jnp.where(tri(), dot(q, k, NT), 0.0).astype(BF)
            out[:, head(h)] = scale * (dot(q, prefix[h]) + dot(sc, v))

    whole_rows = rows % LANE == 0

    def add(acc, buf, ctx):
        if not whole_rows:
            return
        at = pl.ds(pl.multiple_of(ctx * rows, LANE), rows)
        acc[...] += dot(tbuf[0, :, at], buf[0, at, :]) + dot(tbuf[1, :, at], buf[1, at, :])

    def add_ring(s):
        add(tcw, wcw, ctx_of(pos - s))
        add(tccw, wccw, ctx_of(pos + s))

    def add_y(s):
        y_in = y_copy(s)
        y_in.wait_recv()
        add(ty, wy, ctx_of(pos + s))

    for acc in (tcw, tccw, ty):
        acc[...] = jnp.zeros_like(acc)
    for copy in local:
        copy.wait()
    for copy in first:
        copy.wait_recv()
    cw_copy(0).start()
    cc_copy(0).start()

    @pl.when(me == 0)
    def _():
        xbuf[pl.ds(0, taps), :] = jnp.zeros((taps, chans), BF)

    mix()

    @pl.when(me + 1 < n)
    def _():
        halo.start()

    own_state()
    scan_send(0, *fwd)
    nblk = toks // taps

    def work1():
        conv(range(1, nblk))

    def work2():
        @pl.when(me >= 1)
        def _():
            halo.wait_recv()

        conv(range(1))
        tcopy.start()

    def work3():
        for k in range(rounds):
            scan_recv(k, *fwd)
            if k + 1 < rounds:
                scan_send(k + 1, *fwd)
        forward()

    def work4():
        tcopy.wait_recv()
        add(tcw, wcw, me)
        add(tccw, wccw, me)
        add(ty, wy, me)
        for s in range(1, 5):
            add_ring(s)
        for s in range(1, 4):
            add_y(s)

    works = {1: work1, 2: work2, 3: work3, 4: work4}
    for s in range(1, 5):
        ring_in(s)
        works[s]()

    @pl.loop(5, n)
    def _(s):
        ring_in(s)
        add_ring(s)
        add_y(s - 1)

    add_y(n - 1)
    if not whole_rows:
        for acc, buf in ((tcw, wcw), (tccw, wccw), (ty, wy)):

            @pl.loop(0, chans // 256)
            def _(c):
                at = pl.ds(pl.multiple_of(c * 256, 256), 256)
                acc[...] += dot(tbuf[0, :, at], buf[0, at, :]) + dot(tbuf[1, :, at], buf[1, at, :])

    def put(at, target):
        resid[:, at] = (tokw[...] * (out[:, at] - target)).astype(BF)

    put(pl.ds(common, cwn), tcw[...])
    put(pl.ds(common + cwn, LANE), tccw[:, :LANE])
    put(pl.ds(pl.multiple_of(g * quarter, LANE), quarter), tccw[:, LANE:])
    put(pl.ds(pl.multiple_of((1 - g) * quarter, LANE), quarter), ty[...])

    exc[...] = jnp.zeros_like(exc)

    @pl.loop(0, heads)
    def _(h):
        own[h] = dot(qkv[0, :, head(h)], resid[:, head(h)], TN)

    scan_send(0, *bwd)

    @pl.loop(0, heads)
    def _(h):
        q, k, v = qkv[0, :, head(h)], qkv[1, :, head(h)], qkv[2, :, head(h)]
        rs = resid[:, head(h)]
        gs = jnp.where(tri(), dot(rs, v, NT), 0.0).astype(BF)
        grads[0, :, head(h)] = (scale * (dot(rs, prefix[h], NT) + dot(gs, k))).astype(BF)
        out[:, head(h)] = dot(gs, q, TN)

    for k in range(rounds):
        scan_recv(k, *bwd)
        if k + 1 < rounds:
            scan_send(k + 1, *bwd)

    @pl.loop(0, heads)
    def _(h):
        q, k, v = qkv[0, :, head(h)], qkv[1, :, head(h)], qkv[2, :, head(h)]
        later = exc[h].astype(BF)
        sc = jnp.where(tri(), dot(q, k, NT), 0.0).astype(BF)
        grads[1, :, head(h)] = (scale * (dot(v, later, NT) + out[:, head(h)])).astype(BF)
        grads[2, :, head(h)] = (scale * (dot(k, later) + dot(sc, resid[:, head(h)], TN))).astype(BF)

    for copy in first:
        copy.wait_send()

    @pl.when(me + 1 < n)
    def _():
        halo.wait_send()

    tcopy.wait_send()
    for k in range(rounds):
        scan_done(k, *fwd)
        scan_done(k, *bwd)

    @pl.loop(0, n - 1)
    def _(s):
        cw_copy(s).wait_send()
        cc_copy(s).wait_send()
        y_copy(s + 1).wait_send()


def on_device(n, teacher_streams, conv_filter, map_weight, bases, base_weights, student_qkv):
    toks, chans = teacher_streams.shape[1:]
    width = student_qkv.shape[2]
    heads = width // DH
    nx = 4 if n % 64 == 0 else 2
    rounds = max(1, (n - 1).bit_length())
    scale = float(DH * toks * n) ** (-0.5)
    onehot = (bases[:, None] == jnp.arange(base_weights.shape[0])[None, :]).astype(F32)
    tokw = jnp.sum(onehot * base_weights[None, :], axis=1, keepdims=True)
    consts = [jnp.asarray(m) for m in transform(conv_filter.shape[1])]
    cwn = width // 2 - LANE
    ccn = width // 4 + LANE
    quarter = width // 4
    dma = pltpu.SemaphoreType.DMA
    state = (rounds, heads, DH, DH)
    scratch = [
        pltpu.VMEM((2, chans, cwn), BF),
        pltpu.VMEM((2, chans, ccn), BF),
        pltpu.VMEM((2, chans, quarter), BF),
        pltpu.VMEM((toks + conv_filter.shape[1], chans), BF),
        pltpu.VMEM((2, toks, chans), BF),
        pltpu.VMEM((toks, cwn), F32),
        pltpu.VMEM((toks, ccn), F32),
        pltpu.VMEM((toks, quarter), F32),
        pltpu.VMEM((toks, width), F32),
        pltpu.VMEM((toks, width), BF),
        pltpu.VMEM((heads, DH, DH), F32),
        pltpu.VMEM((heads, DH, DH), F32),
        pltpu.VMEM((heads, DH, DH), BF),
        pltpu.VMEM(state, BF),
        pltpu.VMEM(state, BF),
        pltpu.VMEM(state, BF),
        pltpu.VMEM(state, BF),
        dma((4,)), dma((4,)), dma((4,)),
        dma((n,)), dma((n,)), dma((n,)), dma((n,)), dma((n,)), dma((n,)),
        dma, dma, dma, dma,
        dma((rounds,)), dma((rounds,)), dma((rounds,)), dma((rounds,)),
    ]
    vmem = pl.BlockSpec(memory_space=pltpu.VMEM)
    return pl.pallas_call(
        functools.partial(kernel, n, nx, scale),
        out_shape=jax.ShapeDtypeStruct((3, toks, width), BF),
        in_specs=[vmem] * 9,
        out_specs=vmem,
        scratch_shapes=scratch,
        compiler_params=pltpu.CompilerParams(
            collective_id=0, has_side_effects=True, vmem_limit_bytes=56 * 1024 * 1024
        ),
    )(teacher_streams, conv_filter, map_weight, tokw, student_qkv, *consts)


def solution(mesh):
    in_specs = (
        P(None, ("grp", "ctx"), "role"),
        P("role", None),
        P(("role", "ctx"), None),
        P(("grp", "ctx")),
        P(),
        P(None, ("grp", "ctx"), "role"),
    )
    out_specs = P(None, ("grp", "ctx"), "role")
    return jax.shard_map(
        functools.partial(on_device, mesh.shape["ctx"]),
        mesh=mesh,
        in_specs=in_specs,
        out_specs=out_specs,
        check_vma=False,
    )
```

```python
import functools

import jax
import jax.numpy as jnp
import ml_dtypes
import numpy as np
from jax import lax
from jax.experimental import pallas as pl
from jax.experimental.pallas import tpu as pltpu
from jax.sharding import PartitionSpec as P

DH = 128
LANE = 128
BF = jnp.bfloat16
F32 = jnp.float32
MESH = pl.DeviceIdType.MESH


def transform(taps):
    freq = np.arange(taps)[:, None]
    time = np.arange(2 * taps)[None, :]
    angle = np.pi * ((2 * freq + 1) * time % (4 * taps)) / (2 * taps)
    full = np.concatenate([np.cos(angle), -np.sin(angle)], 0)
    back = full[:, taps:].T / taps
    pieces = []
    for matrix in (full, back):
        high = matrix.astype(ml_dtypes.bfloat16)
        low = (matrix - high.astype(np.float64)).astype(ml_dtypes.bfloat16)
        pieces += [high, low]
    return pieces


def dot(a, b, dims=((1,), (0,))):
    return lax.dot_general(a, b, (dims, ((), ())), preferred_element_type=F32)


NT = ((1,), (1,))
TN = ((0,), (0,))


def kernel(
    n, nx, scale,
    streams_in, filt, wmap, tokw, qkv, fhi, flo, ghi, glo,
    grads,
    streams, hbuf, wcw, wccw, wy, xbuf, tbuf, tcw, tccw, ty, out, resid, own, exc, prefix, hsend, hrecv, bsend, brecv,
    st_sem, in_loc, in_send, in_recv, cw_send, cw_recv, cc_send, cc_recv, y_send, y_recv,
    halo_send, halo_recv, t_send, t_recv, h_ssem, h_rsem, b_ssem, b_rsem,
):
    toks, chans = streams.shape[1], streams.shape[2]
    width = qkv.shape[2]
    heads = width // DH
    rows = wmap.shape[0]
    taps = filt.shape[1]
    rounds = hsend.shape[0]
    quarter = width // 4
    cwn = tcw.shape[1]
    common = width // 2
    g, r, me = lax.axis_index("grp"), lax.axis_index("role"), lax.axis_index("ctx")
    nz = n // nx

    def ctx_of(pos):
        pos = lax.rem(pos + n, n)
        x, t = lax.div(pos, nz), lax.rem(pos, nz)
        z = t + lax.rem(x, 2) * (nz - 1 - 2 * t)
        return z * nx + x

    z0, x0 = lax.div(me, nx), lax.rem(me, nx)
    pos = x0 * nz + z0 + lax.rem(x0, 2) * (nz - 1 - 2 * z0)
    nxt, prv = ctx_of(pos + 1), ctx_of(pos - 1)

    bar = pltpu.get_barrier_semaphore()
    for peer in ({"ctx": nxt}, {"ctx": prv}, {"grp": 1 - g}, {"role": 1 - r}):
        pl.semaphore_signal(bar, inc=1, device_id=peer, device_id_type=MESH)
    for k in range(rounds):
        d = 1 << k

        @pl.when(me + d < n)
        def _():
            pl.semaphore_signal(bar, inc=1, device_id={"ctx": me + d}, device_id_type=MESH)

        @pl.when(me >= d)
        def _():
            pl.semaphore_signal(bar, inc=1, device_id={"ctx": me - d}, device_id_type=MESH)

    peers = 4
    for k in range(rounds):
        d = 1 << k
        peers = peers + jnp.where(me + d < n, 1, 0) + jnp.where(me >= d, 1, 0)
    pl.semaphore_wait(bar, peers)

    def span(ctx):
        return pl.ds(pl.multiple_of(ctx * rows, 16), rows)

    def remote(src, dst, ssem, rsem, peer):
        return pltpu.make_async_remote_copy(
            src_ref=src, dst_ref=dst, send_sem=ssem, recv_sem=rsem, device_id=peer, device_id_type=MESH
        )

    def shares(role):
        base = role * width
        mine = base + g * quarter
        other = base + (1 - g) * quarter
        cols = lambda at, size: pl.ds(pl.multiple_of(at, LANE), size)
        return [
            (wmap.at[:, cols(base + common, cwn)], wcw.at[r, span(me), :]),
            (wmap.at[:, cols(base + common + cwn, LANE)], wccw.at[r, span(me), pl.ds(0, LANE)]),
            (wmap.at[:, cols(mine, quarter)], wccw.at[r, span(me), pl.ds(LANE, quarter)]),
            (wmap.at[:, cols(other, quarter)], wy.at[r, span(me), :]),
        ]

    first = [
        remote(src, dst, in_send.at[i], in_recv.at[i], {"role": 1 - r})
        for i, (src, dst) in enumerate(shares(1 - r))
    ]
    for copy in first:
        copy.start()
    fetch = pltpu.make_async_copy(streams_in, streams, st_sem)
    fetch.start()
    local = [
        pltpu.make_async_copy(src, dst, in_loc.at[i]) for i, (src, dst) in enumerate(shares(r))
    ]
    for copy in local:
        copy.start()

    def move(src, dst, ctx, part, ssem, rsem, s, peer):
        at = span(ctx)
        return remote(src.at[part, at, :], dst.at[part, at, :], ssem.at[s, part], rsem.at[s, part], peer)

    def cw_copy(s, part):
        return move(wcw, wcw, ctx_of(pos - s), part, cw_send, cw_recv, s, {"ctx": nxt})

    def cw_in(s, part):
        return move(wcw, wcw, ctx_of(pos - s), part, cw_send, cw_recv, s - 1, {"ctx": nxt})

    def cc_copy(s, part):
        return move(wccw, wccw, ctx_of(pos + s), part, cc_send, cc_recv, s, {"ctx": prv})

    def cc_in(s, part):
        return move(wccw, wccw, ctx_of(pos + s), part, cc_send, cc_recv, s - 1, {"ctx": prv})

    def y_copy(s, part):
        at = span(ctx_of(pos + s))
        return remote(
            wccw.at[part, at, pl.ds(LANE, quarter)],
            wy.at[part, at, :],
            y_send.at[s, part],
            y_recv.at[s, part],
            {"grp": 1 - g},
        )

    def ring_in(s, part):
        def go(arrived, copy):
            arrived.wait_recv()
            if not isinstance(s, int):
                pl.when(s < n - 1)(lambda: copy(s, part).start())
            elif s < n - 1:
                copy(s, part).start()

        go(cw_in(s, part), cw_copy)
        go(cc_in(s, part), cc_copy)
        y_copy(s, part).start()

    def mix():
        @pl.loop(0, toks // 128)
        def _(b):
            at = pl.ds(pl.multiple_of(b * 128, 128), 128)
            xbuf[pl.ds(pl.multiple_of(b * 128 + taps, 128), 128), :] = (
                streams[1, at, :].astype(F32) * streams[2, at, :].astype(F32)
            ).astype(BF)

    halo = remote(
        xbuf.at[pl.ds(toks, taps), :], xbuf.at[pl.ds(0, taps), :], halo_send, halo_recv, {"ctx": me + 1}
    )

    def head(h):
        return pl.ds(pl.multiple_of(h * DH, DH), DH)

    def scan_send(k, up, send, recv, ssem, rsem):
        d = 1 << k
        send[k] = (own[...] + exc[...]).astype(BF)

        @pl.when((me + d < n) if up else (me >= d))
        def _():
            scan_copy(k, up, send, recv, ssem, rsem).start()

    def scan_copy(k, up, send, recv, ssem, rsem):
        d = 1 << k
        return remote(send.at[k], recv.at[k], ssem.at[k], rsem.at[k], {"ctx": me + d if up else me - d})

    def scan_recv(k, up, send, recv, ssem, rsem):
        d = 1 << k

        @pl.when((me >= d) if up else (me + d < n))
        def _():
            scan_copy(k, up, send, recv, ssem, rsem).wait_recv()
            exc[...] += recv[k].astype(F32)

    def scan_done(k, up, send, recv, ssem, rsem):
        d = 1 << k

        @pl.when((me + d < n) if up else (me >= d))
        def _():
            scan_copy(k, up, send, recv, ssem, rsem).wait_send()

    fwd = (True, hsend, hrecv, h_ssem, h_rsem)
    bwd = (False, bsend, brecv, b_ssem, b_rsem)

    def own_state():
        exc[...] = jnp.zeros_like(exc)

        @pl.loop(0, heads)
        def _(h):
            own[h] = dot(qkv[1, :, head(h)], qkv[2, :, head(h)], TN)

    tile = 256

    def filters():
        @pl.loop(0, chans // tile)
        def _(c):
            cols = pl.ds(pl.multiple_of(c * tile, tile), tile)
            taps_c = filt[cols, :]
            hbuf[:, cols] = dot(fhi[:, :taps], taps_c, NT) + dot(flo[:, :taps], taps_c, NT)

    def conv(b):
        @pl.loop(0, chans // tile)
        def _(c):
            cols = pl.ds(pl.multiple_of(c * tile, tile), tile)
            hr, hi = hbuf[:taps, cols], hbuf[taps:, cols]
            x = xbuf[b * taps : (b + 2) * taps, cols]
            xx = dot(fhi[...], x) + dot(flo[...], x)
            xr, xi = xx[:taps], xx[taps:]
            y = jnp.concatenate([xr * hr - xi * hi, xr * hi + xi * hr], 0)
            yh = y.astype(BF)
            yl = (y - yh.astype(F32)).astype(BF)
            res = dot(ghi[...], yh) + dot(ghi[...], yl) + dot(glo[...], yh)
            at = pl.ds(b * taps, taps)
            tbuf[r, at, cols] = (streams[0, at, cols].astype(F32) * res).astype(BF)

    tcopy = remote(tbuf.at[r], tbuf.at[r], t_send, t_recv, {"role": 1 - r})

    def tri():
        return lax.broadcasted_iota(jnp.int32, (toks, toks), 0) >= lax.broadcasted_iota(
            jnp.int32, (toks, toks), 1
        )

    def inside(low, high):
        @pl.loop(low, high)
        def _(h):
            q, k, v = qkv[0, :, head(h)], qkv[1, :, head(h)], qkv[2, :, head(h)]
            sc = jnp.where(tri(), dot(q, k, NT), 0.0).astype(BF)
            out[:, head(h)] = dot(sc, v)

    def outside():
        prefix[...] = exc[...].astype(BF)

        @pl.loop(0, heads)
        def _(h):
            out[:, head(h)] = scale * (dot(qkv[0, :, head(h)], prefix[h]) + out[:, head(h)])

    whole_rows = rows % LANE == 0

    def add(acc, buf, ctx):
        if not whole_rows:
            return
        at = pl.ds(pl.multiple_of(ctx * rows, LANE), rows)
        acc[...] += dot(tbuf[0, :, at], buf[0, at, :]) + dot(tbuf[1, :, at], buf[1, at, :])

    def add_ring(s):
        add(tcw, wcw, ctx_of(pos - s))
        add(tccw, wccw, ctx_of(pos + s))

    def add_y(s):
        for part in range(2):
            y_copy(s, part).wait_recv()
        add(ty, wy, ctx_of(pos + s))

    for copy in local:
        copy.wait()
    for copy in first:
        copy.wait_recv()
    for part in range(2):
        cw_copy(0, part).start()
        cc_copy(0, part).start()

    @pl.when(me == 0)
    def _():
        xbuf[pl.ds(0, taps), :] = jnp.zeros((taps, chans), BF)

    fetch.wait()
    mix()

    @pl.when(me + 1 < n)
    def _():
        halo.start()

    own_state()
    scan_send(0, *fwd)
    filters()
    for acc in (tcw, tccw, ty):
        acc[...] = jnp.zeros_like(acc)
    nblk = toks // taps

    def halo_in():
        @pl.when(me >= 1)
        def _():
            halo.wait_recv()

    def scan_step(k):
        if k < rounds:
            scan_recv(k, *fwd)
            if k + 1 < rounds:
                scan_send(k + 1, *fwd)

    def own_share():
        tcopy.wait_recv()
        add(tcw, wcw, me)
        add(tccw, wccw, me)
        add(ty, wy, me)

    def last_scans():
        for k in range(4, rounds):
            scan_step(k)

    works = {
        (1, 0): [lambda: conv(1)],
        (1, 1): [lambda: conv(2)],
        (2, 0): [lambda: [conv(b) for b in range(3, nblk)]],
        (2, 1): [halo_in, lambda: conv(0), tcopy.start],
        (3, 0): [lambda: scan_step(0), lambda: inside(0, heads // 2)],
        (3, 1): [lambda: inside(heads // 2, heads)],
        (4, 0): [lambda: scan_step(1), own_share],
        (4, 1): [lambda: add_ring(1)],
        (5, 0): [lambda: scan_step(2), lambda: add_ring(2), lambda: add_y(1)],
        (5, 1): [lambda: add_ring(3), lambda: add_y(2)],
        (6, 0): [lambda: scan_step(3), lambda: add_ring(4), lambda: add_y(3)],
        (6, 1): [lambda: add_ring(5), lambda: add_y(4)],
        (7, 0): [last_scans, outside, lambda: add_ring(6), lambda: add_y(5)],
        (7, 1): [lambda: add_y(6), lambda: add_ring(7)],
    }
    for s in range(1, 8):
        for part in range(2):
            ring_in(s, part)
            for work in works[s, part]:
                work()

    @pl.loop(8, n)
    def _(s):
        for part in range(2):
            ring_in(s, part)
        add_ring(s)
        add_y(s - 1)

    add_y(n - 1)
    if not whole_rows:
        for acc, buf in ((tcw, wcw), (tccw, wccw), (ty, wy)):

            @pl.loop(0, chans // 256)
            def _(c):
                at = pl.ds(pl.multiple_of(c * 256, 256), 256)
                acc[...] += dot(tbuf[0, :, at], buf[0, at, :]) + dot(tbuf[1, :, at], buf[1, at, :])

    def put(at, target):
        resid[:, at] = (tokw[...] * (out[:, at] - target)).astype(BF)

    put(pl.ds(common, cwn), tcw[...])
    put(pl.ds(common + cwn, LANE), tccw[:, :LANE])
    put(pl.ds(pl.multiple_of(g * quarter, LANE), quarter), tccw[:, LANE:])
    put(pl.ds(pl.multiple_of((1 - g) * quarter, LANE), quarter), ty[...])

    exc[...] = jnp.zeros_like(exc)

    @pl.loop(0, heads)
    def _(h):
        own[h] = dot(qkv[0, :, head(h)], resid[:, head(h)], TN)

    scan_send(0, *bwd)

    @pl.loop(0, heads)
    def _(h):
        q, k, v = qkv[0, :, head(h)], qkv[1, :, head(h)], qkv[2, :, head(h)]
        rs = resid[:, head(h)]
        gs = jnp.where(tri(), dot(rs, v, NT), 0.0).astype(BF)
        grads[0, :, head(h)] = (scale * (dot(rs, prefix[h], NT) + dot(gs, k))).astype(BF)
        out[:, head(h)] = dot(gs, q, TN)

    for k in range(rounds):
        scan_recv(k, *bwd)
        if k + 1 < rounds:
            scan_send(k + 1, *bwd)

    @pl.loop(0, heads)
    def _(h):
        q, k, v = qkv[0, :, head(h)], qkv[1, :, head(h)], qkv[2, :, head(h)]
        later = exc[h].astype(BF)
        sc = jnp.where(tri(), dot(q, k, NT), 0.0).astype(BF)
        grads[1, :, head(h)] = (scale * (dot(v, later, NT) + out[:, head(h)])).astype(BF)
        grads[2, :, head(h)] = (scale * (dot(k, later) + dot(sc, resid[:, head(h)], TN))).astype(BF)

    for copy in first:
        copy.wait_send()

    @pl.when(me + 1 < n)
    def _():
        halo.wait_send()

    tcopy.wait_send()
    for k in range(rounds):
        scan_done(k, *fwd)
        scan_done(k, *bwd)

    @pl.loop(0, n - 1)
    def _(s):
        for part in range(2):
            cw_copy(s, part).wait_send()
            cc_copy(s, part).wait_send()
            y_copy(s + 1, part).wait_send()


def on_device(n, teacher_streams, conv_filter, map_weight, bases, base_weights, student_qkv):
    toks, chans = teacher_streams.shape[1:]
    width = student_qkv.shape[2]
    heads = width // DH
    nx = 4 if n % 64 == 0 else 2
    rounds = max(1, (n - 1).bit_length())
    scale = float(DH * toks * n) ** (-0.5)
    onehot = (bases[:, None] == jnp.arange(base_weights.shape[0])[None, :]).astype(F32)
    tokw = jnp.sum(onehot * base_weights[None, :], axis=1, keepdims=True)
    consts = [jnp.asarray(m) for m in transform(conv_filter.shape[1])]
    cwn = width // 2 - LANE
    ccn = width // 4 + LANE
    quarter = width // 4
    dma = pltpu.SemaphoreType.DMA
    state = (rounds, heads, DH, DH)
    scratch = [
        pltpu.VMEM(teacher_streams.shape, BF),
        pltpu.VMEM((2 * conv_filter.shape[1], chans), F32),
        pltpu.VMEM((2, chans, cwn), BF),
        pltpu.VMEM((2, chans, ccn), BF),
        pltpu.VMEM((2, chans, quarter), BF),
        pltpu.VMEM((toks + conv_filter.shape[1], chans), BF),
        pltpu.VMEM((2, toks, chans), BF),
        pltpu.VMEM((toks, cwn), F32),
        pltpu.VMEM((toks, ccn), F32),
        pltpu.VMEM((toks, quarter), F32),
        pltpu.VMEM((toks, width), F32),
        pltpu.VMEM((toks, width), BF),
        pltpu.VMEM((heads, DH, DH), F32),
        pltpu.VMEM((heads, DH, DH), F32),
        pltpu.VMEM((heads, DH, DH), BF),
        pltpu.VMEM(state, BF),
        pltpu.VMEM(state, BF),
        pltpu.VMEM(state, BF),
        pltpu.VMEM(state, BF),
        dma, dma((4,)), dma((4,)), dma((4,)),
        dma((n, 2)), dma((n, 2)), dma((n, 2)), dma((n, 2)), dma((n, 2)), dma((n, 2)),
        dma, dma, dma, dma,
        dma((rounds,)), dma((rounds,)), dma((rounds,)), dma((rounds,)),
    ]
    vmem = pl.BlockSpec(memory_space=pltpu.VMEM)
    return pl.pallas_call(
        functools.partial(kernel, n, nx, scale),
        out_shape=jax.ShapeDtypeStruct((3, toks, width), BF),
        in_specs=[pl.BlockSpec(memory_space=pl.ANY)] + [vmem] * 8,
        out_specs=vmem,
        scratch_shapes=scratch,
        compiler_params=pltpu.CompilerParams(
            collective_id=0, has_side_effects=True, vmem_limit_bytes=56 * 1024 * 1024
        ),
    )(teacher_streams, conv_filter, map_weight, tokw, student_qkv, *consts)


def solution(mesh):
    in_specs = (
        P(None, ("grp", "ctx"), "role"),
        P("role", None),
        P(("role", "ctx"), None),
        P(("grp", "ctx")),
        P(),
        P(None, ("grp", "ctx"), "role"),
    )
    out_specs = P(None, ("grp", "ctx"), "role")
    return jax.shard_map(
        functools.partial(on_device, mesh.shape["ctx"]),
        mesh=mesh,
        in_specs=in_specs,
        out_specs=out_specs,
        check_vma=False,
    )
```

```python
import functools

import jax
import jax.numpy as jnp
import ml_dtypes
import numpy as np
from jax import lax
from jax.experimental import pallas as pl
from jax.experimental.pallas import tpu as pltpu
from jax.sharding import PartitionSpec as P

DH = 128
LANE = 128
BF = jnp.bfloat16
F32 = jnp.float32
MESH = pl.DeviceIdType.MESH


def transform(taps):
    freq = np.arange(taps)[:, None]
    time = np.arange(2 * taps)[None, :]
    angle = np.pi * ((2 * freq + 1) * time % (4 * taps)) / (2 * taps)
    full = np.concatenate([np.cos(angle), -np.sin(angle)], 0)
    back = full[:, taps:].T / taps
    pieces = []
    for matrix in (full, back):
        high = matrix.astype(ml_dtypes.bfloat16)
        low = (matrix - high.astype(np.float64)).astype(ml_dtypes.bfloat16)
        pieces += [high, low]
    return pieces


def dot(a, b, dims=((1,), (0,))):
    return lax.dot_general(a, b, (dims, ((), ())), preferred_element_type=F32)


NT = ((1,), (1,))
TN = ((0,), (0,))


def kernel(
    n, nx, scale,
    streams_in, filt, wmap, tokw, qkv, fhi, flo, ghi, glo,
    grads,
    streams, hbuf, wcw, wccw, wy, xbuf, tbuf, tcw, tccw, ty, out, resid, own, exc, prefix, hsend, hrecv, bsend, brecv,
    st_sem, in_loc, in_send, in_recv, cw_send, cw_recv, cc_send, cc_recv, y_send, y_recv,
    halo_send, halo_recv, t_send, t_recv, h_ssem, h_rsem, b_ssem, b_rsem,
):
    toks, chans = streams.shape[1], streams.shape[2]
    width = qkv.shape[2]
    heads = width // DH
    rows = wmap.shape[0]
    taps = filt.shape[1]
    rounds = hsend.shape[0]
    quarter = width // 4
    cwn = tcw.shape[1]
    common = width // 2
    g, r, me = lax.axis_index("grp"), lax.axis_index("role"), lax.axis_index("ctx")
    nz = n // nx

    def ctx_of(pos):
        pos = lax.rem(pos + n, n)
        x, t = lax.div(pos, nz), lax.rem(pos, nz)
        z = t + lax.rem(x, 2) * (nz - 1 - 2 * t)
        return z * nx + x

    z0, x0 = lax.div(me, nx), lax.rem(me, nx)
    pos = x0 * nz + z0 + lax.rem(x0, 2) * (nz - 1 - 2 * z0)
    nxt, prv = ctx_of(pos + 1), ctx_of(pos - 1)

    bar = pltpu.get_barrier_semaphore()
    for peer in ({"ctx": nxt}, {"ctx": prv}, {"grp": 1 - g}, {"role": 1 - r}):
        pl.semaphore_signal(bar, inc=1, device_id=peer, device_id_type=MESH)
    for k in range(rounds):
        d = 1 << k

        @pl.when(me + d < n)
        def _():
            pl.semaphore_signal(bar, inc=1, device_id={"ctx": me + d}, device_id_type=MESH)

        @pl.when(me >= d)
        def _():
            pl.semaphore_signal(bar, inc=1, device_id={"ctx": me - d}, device_id_type=MESH)

    peers = 4
    for k in range(rounds):
        d = 1 << k
        peers = peers + jnp.where(me + d < n, 1, 0) + jnp.where(me >= d, 1, 0)
    pl.semaphore_wait(bar, peers)

    def span(ctx):
        return pl.ds(pl.multiple_of(ctx * rows, 16), rows)

    def remote(src, dst, ssem, rsem, peer):
        return pltpu.make_async_remote_copy(
            src_ref=src, dst_ref=dst, send_sem=ssem, recv_sem=rsem, device_id=peer, device_id_type=MESH
        )

    def shares(role):
        base = role * width
        mine = base + g * quarter
        other = base + (1 - g) * quarter
        cols = lambda at, size: pl.ds(pl.multiple_of(at, LANE), size)
        return [
            (wmap.at[:, cols(base + common, cwn)], wcw.at[r, span(me), :]),
            (wmap.at[:, cols(base + common + cwn, LANE)], wccw.at[r, span(me), pl.ds(0, LANE)]),
            (wmap.at[:, cols(mine, quarter)], wccw.at[r, span(me), pl.ds(LANE, quarter)]),
            (wmap.at[:, cols(other, quarter)], wy.at[r, span(me), :]),
        ]

    first = [
        remote(src, dst, in_send.at[i], in_recv.at[i], {"role": 1 - r})
        for i, (src, dst) in enumerate(shares(1 - r))
    ]
    for copy in first:
        copy.start()
    fetch = pltpu.make_async_copy(streams_in, streams, st_sem)
    fetch.start()
    local = [
        pltpu.make_async_copy(src, dst, in_loc.at[i]) for i, (src, dst) in enumerate(shares(r))
    ]
    for copy in local:
        copy.start()

    def move(src, dst, ctx, part, ssem, rsem, s, peer):
        at = span(ctx)
        return remote(src.at[part, at, :], dst.at[part, at, :], ssem.at[s, part], rsem.at[s, part], peer)

    def cw_copy(s, part):
        return move(wcw, wcw, ctx_of(pos - s), part, cw_send, cw_recv, s, {"ctx": nxt})

    def cw_in(s, part):
        return move(wcw, wcw, ctx_of(pos - s), part, cw_send, cw_recv, s - 1, {"ctx": nxt})

    def cc_copy(s, part):
        return move(wccw, wccw, ctx_of(pos + s), part, cc_send, cc_recv, s, {"ctx": prv})

    def cc_in(s, part):
        return move(wccw, wccw, ctx_of(pos + s), part, cc_send, cc_recv, s - 1, {"ctx": prv})

    def y_copy(s, part):
        at = span(ctx_of(pos + s))
        return remote(
            wccw.at[part, at, pl.ds(LANE, quarter)],
            wy.at[part, at, :],
            y_send.at[s, part],
            y_recv.at[s, part],
            {"grp": 1 - g},
        )

    def ring_in(s, part):
        def go(arrived, copy):
            arrived.wait_recv()
            if not isinstance(s, int):
                pl.when(s < n - 1)(lambda: copy(s, part).start())
            elif s < n - 1:
                copy(s, part).start()

        go(cw_in(s, part), cw_copy)
        go(cc_in(s, part), cc_copy)
        y_copy(s, part).start()

    def mix():
        @pl.loop(0, toks // 128)
        def _(b):
            at = pl.ds(pl.multiple_of(b * 128, 128), 128)
            xbuf[pl.ds(pl.multiple_of(b * 128 + taps, 128), 128), :] = (
                streams[1, at, :].astype(F32) * streams[2, at, :].astype(F32)
            ).astype(BF)

    halo = remote(
        xbuf.at[pl.ds(toks, taps), :], xbuf.at[pl.ds(0, taps), :], halo_send, halo_recv, {"ctx": me + 1}
    )

    def head(h):
        return pl.ds(pl.multiple_of(h * DH, DH), DH)

    def scan_send(k, up, send, recv, ssem, rsem):
        d = 1 << k
        send[k] = (own[...] + exc[...]).astype(BF)

        @pl.when((me + d < n) if up else (me >= d))
        def _():
            scan_copy(k, up, send, recv, ssem, rsem).start()

    def scan_copy(k, up, send, recv, ssem, rsem):
        d = 1 << k
        return remote(send.at[k], recv.at[k], ssem.at[k], rsem.at[k], {"ctx": me + d if up else me - d})

    def scan_recv(k, up, send, recv, ssem, rsem):
        d = 1 << k

        @pl.when((me >= d) if up else (me + d < n))
        def _():
            scan_copy(k, up, send, recv, ssem, rsem).wait_recv()
            exc[...] += recv[k].astype(F32)

    def scan_done(k, up, send, recv, ssem, rsem):
        d = 1 << k

        @pl.when((me + d < n) if up else (me >= d))
        def _():
            scan_copy(k, up, send, recv, ssem, rsem).wait_send()

    fwd = (True, hsend, hrecv, h_ssem, h_rsem)
    bwd = (False, bsend, brecv, b_ssem, b_rsem)

    def own_state():
        exc[...] = jnp.zeros_like(exc)

        @pl.loop(0, heads)
        def _(h):
            own[h] = dot(qkv[1, :, head(h)], qkv[2, :, head(h)], TN)

    tile = 256

    def filters():
        @pl.loop(0, chans // tile)
        def _(c):
            cols = pl.ds(pl.multiple_of(c * tile, tile), tile)
            taps_c = filt[cols, :]
            hbuf[:, cols] = dot(fhi[:, :taps], taps_c, NT) + dot(flo[:, :taps], taps_c, NT)

    def conv(b):
        @pl.loop(0, chans // tile)
        def _(c):
            cols = pl.ds(pl.multiple_of(c * tile, tile), tile)
            hr, hi = hbuf[:taps, cols], hbuf[taps:, cols]
            x = xbuf[b * taps : (b + 2) * taps, cols]
            xx = dot(fhi[...], x) + dot(flo[...], x)
            xr, xi = xx[:taps], xx[taps:]
            y = jnp.concatenate([xr * hr - xi * hi, xr * hi + xi * hr], 0)
            yh = y.astype(BF)
            yl = (y - yh.astype(F32)).astype(BF)
            res = dot(ghi[...], yh) + dot(ghi[...], yl) + dot(glo[...], yh)
            at = pl.ds(b * taps, taps)
            tbuf[r, at, cols] = (streams[0, at, cols].astype(F32) * res).astype(BF)

    tcopy = remote(tbuf.at[r], tbuf.at[r], t_send, t_recv, {"role": 1 - r})

    def tri():
        return lax.broadcasted_iota(jnp.int32, (toks, toks), 0) >= lax.broadcasted_iota(
            jnp.int32, (toks, toks), 1
        )

    def inside(low, high):
        @pl.loop(low, high)
        def _(h):
            q, k, v = qkv[0, :, head(h)], qkv[1, :, head(h)], qkv[2, :, head(h)]
            sc = jnp.where(tri(), dot(q, k, NT), 0.0).astype(BF)
            out[:, head(h)] = dot(sc, v)

    def outside():
        prefix[...] = exc[...].astype(BF)

        @pl.loop(0, heads)
        def _(h):
            out[:, head(h)] = scale * (dot(qkv[0, :, head(h)], prefix[h]) + out[:, head(h)])

    whole_rows = rows % LANE == 0

    def add(acc, buf, ctx):
        if not whole_rows:
            return
        at = pl.ds(pl.multiple_of(ctx * rows, LANE), rows)
        acc[...] += dot(tbuf[0, :, at], buf[0, at, :]) + dot(tbuf[1, :, at], buf[1, at, :])

    def add_ring(s):
        add(tcw, wcw, ctx_of(pos - s))
        add(tccw, wccw, ctx_of(pos + s))

    def add_y(s):
        for part in range(2):
            y_copy(s, part).wait_recv()
        add(ty, wy, ctx_of(pos + s))

    for copy in local:
        copy.wait()
    for copy in first:
        copy.wait_recv()
    for part in range(2):
        cw_copy(0, part).start()
        cc_copy(0, part).start()

    @pl.when(me == 0)
    def _():
        xbuf[pl.ds(0, taps), :] = jnp.zeros((taps, chans), BF)

    fetch.wait()
    mix()

    @pl.when(me + 1 < n)
    def _():
        halo.start()

    own_state()
    scan_send(0, *fwd)
    filters()
    for acc in (tcw, tccw, ty):
        acc[...] = jnp.zeros_like(acc)
    nblk = toks // taps

    def halo_in():
        @pl.when(me >= 1)
        def _():
            halo.wait_recv()

    def scan_step(k):
        if k < rounds:
            scan_recv(k, *fwd)
            if k + 1 < rounds:
                scan_send(k + 1, *fwd)

    def own_share():
        tcopy.wait_recv()
        add(tcw, wcw, me)
        add(tccw, wccw, me)
        add(ty, wy, me)

    def last_scans():
        for k in range(2, rounds):
            scan_step(k)

    works = {
        (1, 0): [lambda: conv(1)],
        (1, 1): [lambda: conv(2)],
        (2, 0): [lambda: [conv(b) for b in range(3, nblk)]],
        (2, 1): [halo_in, lambda: conv(0), tcopy.start],
        (3, 0): [lambda: inside(0, heads // 2)],
        (3, 1): [lambda: scan_step(0), lambda: inside(heads // 2, heads)],
        (4, 0): [own_share],
        (4, 1): [lambda: add_ring(1)],
        (5, 0): [lambda: scan_step(1), lambda: add_ring(2), lambda: add_y(1)],
        (5, 1): [lambda: add_ring(3), lambda: add_y(2)],
        (6, 0): [lambda: add_ring(4), lambda: add_y(3)],
        (6, 1): [lambda: add_ring(5), lambda: add_y(4)],
        (7, 0): [lambda: add_ring(6), lambda: add_y(5)],
        (7, 1): [last_scans, outside, lambda: add_y(6), lambda: add_ring(7)],
    }
    for s in range(1, 8):
        for part in range(2):
            ring_in(s, part)
            for work in works[s, part]:
                work()

    @pl.loop(8, n)
    def _(s):
        for part in range(2):
            ring_in(s, part)
        add_ring(s)
        add_y(s - 1)

    add_y(n - 1)
    if not whole_rows:
        for acc, buf in ((tcw, wcw), (tccw, wccw), (ty, wy)):

            @pl.loop(0, chans // 256)
            def _(c):
                at = pl.ds(pl.multiple_of(c * 256, 256), 256)
                acc[...] += dot(tbuf[0, :, at], buf[0, at, :]) + dot(tbuf[1, :, at], buf[1, at, :])

    def put(at, target):
        resid[:, at] = (tokw[...] * (out[:, at] - target)).astype(BF)

    put(pl.ds(common, cwn), tcw[...])
    put(pl.ds(common + cwn, LANE), tccw[:, :LANE])
    put(pl.ds(pl.multiple_of(g * quarter, LANE), quarter), tccw[:, LANE:])
    put(pl.ds(pl.multiple_of((1 - g) * quarter, LANE), quarter), ty[...])

    exc[...] = jnp.zeros_like(exc)

    @pl.loop(0, heads)
    def _(h):
        own[h] = dot(qkv[0, :, head(h)], resid[:, head(h)], TN)

    scan_send(0, *bwd)

    @pl.loop(0, heads)
    def _(h):
        q, k, v = qkv[0, :, head(h)], qkv[1, :, head(h)], qkv[2, :, head(h)]
        rs = resid[:, head(h)]
        gs = jnp.where(tri(), dot(rs, v, NT), 0.0).astype(BF)
        grads[0, :, head(h)] = (scale * (dot(rs, prefix[h], NT) + dot(gs, k))).astype(BF)
        out[:, head(h)] = dot(gs, q, TN)

    for k in range(rounds):
        scan_recv(k, *bwd)
        if k + 1 < rounds:
            scan_send(k + 1, *bwd)

    @pl.loop(0, heads)
    def _(h):
        q, k, v = qkv[0, :, head(h)], qkv[1, :, head(h)], qkv[2, :, head(h)]
        later = exc[h].astype(BF)
        sc = jnp.where(tri(), dot(q, k, NT), 0.0).astype(BF)
        grads[1, :, head(h)] = (scale * (dot(v, later, NT) + out[:, head(h)])).astype(BF)
        grads[2, :, head(h)] = (scale * (dot(k, later) + dot(sc, resid[:, head(h)], TN))).astype(BF)

    for copy in first:
        copy.wait_send()

    @pl.when(me + 1 < n)
    def _():
        halo.wait_send()

    tcopy.wait_send()
    for k in range(rounds):
        scan_done(k, *fwd)
        scan_done(k, *bwd)

    @pl.loop(0, n - 1)
    def _(s):
        for part in range(2):
            cw_copy(s, part).wait_send()
            cc_copy(s, part).wait_send()
            y_copy(s + 1, part).wait_send()


def on_device(n, teacher_streams, conv_filter, map_weight, bases, base_weights, student_qkv):
    toks, chans = teacher_streams.shape[1:]
    width = student_qkv.shape[2]
    heads = width // DH
    nx = 4 if n % 64 == 0 else 2
    rounds = max(1, (n - 1).bit_length())
    scale = float(DH * toks * n) ** (-0.5)
    onehot = (bases[:, None] == jnp.arange(base_weights.shape[0])[None, :]).astype(F32)
    tokw = jnp.sum(onehot * base_weights[None, :], axis=1, keepdims=True)
    consts = [jnp.asarray(m) for m in transform(conv_filter.shape[1])]
    cwn = width // 2 - LANE
    ccn = width // 4 + LANE
    quarter = width // 4
    dma = pltpu.SemaphoreType.DMA
    state = (rounds, heads, DH, DH)
    scratch = [
        pltpu.VMEM(teacher_streams.shape, BF),
        pltpu.VMEM((2 * conv_filter.shape[1], chans), F32),
        pltpu.VMEM((2, chans, cwn), BF),
        pltpu.VMEM((2, chans, ccn), BF),
        pltpu.VMEM((2, chans, quarter), BF),
        pltpu.VMEM((toks + conv_filter.shape[1], chans), BF),
        pltpu.VMEM((2, toks, chans), BF),
        pltpu.VMEM((toks, cwn), F32),
        pltpu.VMEM((toks, ccn), F32),
        pltpu.VMEM((toks, quarter), F32),
        pltpu.VMEM((toks, width), F32),
        pltpu.VMEM((toks, width), BF),
        pltpu.VMEM((heads, DH, DH), F32),
        pltpu.VMEM((heads, DH, DH), F32),
        pltpu.VMEM((heads, DH, DH), BF),
        pltpu.VMEM(state, BF),
        pltpu.VMEM(state, BF),
        pltpu.VMEM(state, BF),
        pltpu.VMEM(state, BF),
        dma, dma((4,)), dma((4,)), dma((4,)),
        dma((n, 2)), dma((n, 2)), dma((n, 2)), dma((n, 2)), dma((n, 2)), dma((n, 2)),
        dma, dma, dma, dma,
        dma((rounds,)), dma((rounds,)), dma((rounds,)), dma((rounds,)),
    ]
    vmem = pl.BlockSpec(memory_space=pltpu.VMEM)
    return pl.pallas_call(
        functools.partial(kernel, n, nx, scale),
        out_shape=jax.ShapeDtypeStruct((3, toks, width), BF),
        in_specs=[pl.BlockSpec(memory_space=pl.ANY)] + [vmem] * 8,
        out_specs=vmem,
        scratch_shapes=scratch,
        compiler_params=pltpu.CompilerParams(
            collective_id=0, has_side_effects=True, vmem_limit_bytes=56 * 1024 * 1024
        ),
    )(teacher_streams, conv_filter, map_weight, tokw, student_qkv, *consts)


def solution(mesh):
    in_specs = (
        P(None, ("grp", "ctx"), "role"),
        P("role", None),
        P(("role", "ctx"), None),
        P(("grp", "ctx")),
        P(),
        P(None, ("grp", "ctx"), "role"),
    )
    out_specs = P(None, ("grp", "ctx"), "role")
    return jax.shard_map(
        functools.partial(on_device, mesh.shape["ctx"]),
        mesh=mesh,
        in_specs=in_specs,
        out_specs=out_specs,
        check_vma=False,
    )
```
